128 devices in a mesh: row: 8 (over z, y_lo), col: 16 (over y_hi, x, core).
Axes of the slice: x: 4, y: 4 (y_hi: 2, y_lo: 2; y = y_hi * 2 + y_lo), z: 4, core: 2. Of those that a mesh axis runs over, the one named last changes fastest.
Arguments:
- hidden: bfloat16 [2048, 26624], P('col', 'row'), may hold values from -6 to 6
- weight: bfloat16 [26624, 8192], P('row', 'col'), may hold values from -0.0546875 to 0.0546875
- grad_out: bfloat16 [2048, 8192], P('row', 'col'), may hold values from -6 to 6
Outputs:
- output: bfloat16 [2048, 8192], P('row', 'col')
- grad_hidden: bfloat16 [2048, 26624], P('col', 'row')
- grad_weight: bfloat16 [26624, 8192], P('row', 'col')
The draws below stay inside these ranges and needn't reach their ends.
All inputs are finite; a program needn't handle non-finite values.
Results may differ from the reference program's by a relative error of at most 0.019.
Values may be sent and summed in bfloat16 or wider, within the bound.
No kernel may reach another device: no remote copies, remote signals or barrier semaphores. Data moves between devices by JAX's collectives and lax.ppermute only.
A program may use at most 128 MiB of HBM per device.

```python
import jax
import jax.numpy as jnp
from jax import lax

D = 8192
FF = 26624
TOKENS = 2048
N_COL = 16


def raised(array, key, source, target, blocks, factor):
    owner, partner = [(jnp.arange(array.shape[dim]) // (array.shape[dim] // blocks)).reshape([-1 if axis == dim else 1 for axis in range(array.ndim)]) for dim in (source, target)]
    chosen = jax.random.permutation(key, blocks)[partner]
    strong = (owner == chosen) | (owner == (partner + blocks // 2) % blocks)
    return jnp.where(strong, factor * array, array)


def levels(key, shape, cuts, smallest, high):
    level = 1.0
    for axis_at, parts in cuts:
        draws = jax.random.uniform(jax.random.fold_in(jax.random.fold_in(key, 6), axis_at), (parts,), jnp.float32, smallest / len(cuts), high / len(cuts))
        level = level * jnp.repeat(jnp.exp(draws), shape[axis_at] // parts).reshape((-1,) + (1,) * (len(shape) - 1 - axis_at))
    return level


def gaussian(stream_key, extent, scale, reach, shards=(), held_as=jnp.bfloat16):
    level = levels(stream_key, extent, shards, -0.22, 0.18) if shards else 1.0
    entries = jax.random.normal(stream_key, extent, jnp.float32) * scale * level
    return jnp.minimum(jnp.maximum(entries, -reach), reach).astype(held_as)


def noise_with(rng, dims, deviation, reach, pieces, heavy, kind=jnp.bfloat16):
    result = deviation * jax.random.normal(rng, dims, jnp.float32)
    if pieces:
        result = result * levels(rng, dims, pieces, -0.22, 0.18)
    return jnp.clip(raised(result, jax.random.fold_in(rng, 3), *heavy), -reach, reach).astype(kind)


def setup_inputs(seed: int = 0) -> dict:
    arg_keys = jax.random.split(jax.random.key(seed), 4)
    hidden = gaussian(arg_keys[0], (TOKENS, FF), 1.0, 6.0, ((0, 16), (1, 8)))
    weight = noise_with(arg_keys[1], (FF, D), FF ** -0.5, 0.0546875, ((0, 8), (1, 16)), (0, 1, 16, 2.0))
    grad_out = noise_with(arg_keys[2], (TOKENS, D), 1.0, 6.0, ((0, 8), (1, 16)), (1, 0, 16, 2.0))
    return dict(hidden=hidden, weight=weight, grad_out=grad_out)


def reference(hidden, weight, grad_out):
    output = jnp.dot(hidden, weight, preferred_element_type=jnp.float32).astype(jnp.bfloat16)
    width = D // N_COL

    def add_block(total, index):
        start = (index * width).astype(jnp.int32)
        cotangent = lax.dynamic_slice_in_dim(grad_out, start, width, 1)
        columns = lax.dynamic_slice_in_dim(weight, start, width, 1)
        part = lax.dot_general(cotangent, columns, (((1,), (1,)), ((), ())), preferred_element_type=jnp.float32)
        part = lax.optimization_barrier(part.astype(jnp.bfloat16))
        return total + part.astype(jnp.float32), None

    start_total = jnp.zeros((hidden.shape[0], hidden.shape[1]), jnp.float32)
    total, _ = lax.scan(add_block, start_total, jnp.arange(N_COL, dtype=jnp.int32))
    grad_hidden = total.astype(jnp.bfloat16)
    grad_weight = lax.dot_general(hidden, grad_out, (((0,), (0,)), ((), ())), preferred_element_type=jnp.float32).astype(jnp.bfloat16)
    return output, grad_hidden, grad_weight
```

```python
import jax
import jax.numpy as jnp
from jax import lax
from jax.sharding import PartitionSpec as P

BF, F32 = jnp.bfloat16, jnp.float32
AXES = ("row", "col")
VIA_Y = 48


def place(row, col):
    z, y_lo = divmod(row, 2)
    y_hi, rest = divmod(col, 8)
    x, core = divmod(rest, 2)
    return x, y_hi, y_lo, z, core


def permutation(move):
    pairs = []
    for row in range(8):
        for col in range(16):
            x, y_hi, y_lo, z, core = move(*place(row, col))
            pairs.append((row * 16 + col, (z % 4 * 2 + y_lo) * 16 + y_hi * 8 + x % 4 * 2 + core))
    return pairs


X1 = permutation(lambda x, yh, yl, z, c: (x + 1 - 2 * c, yh, yl, z, c))
X2 = permutation(lambda x, yh, yl, z, c: (x - 1 + 2 * c, yh, yl, z, c))
Z1 = permutation(lambda x, yh, yl, z, c: (x, yh, yl, z + 1 - 2 * c, c))
Z2 = permutation(lambda x, yh, yl, z, c: (x, yh, yl, z - 1 + 2 * c, c))
YH = permutation(lambda x, yh, yl, z, c: (x, 1 - yh, yl, z, c))
YL = permutation(lambda x, yh, yl, z, c: (x, yh, 1 - yl, z, c))
CORE = permutation(lambda x, yh, yl, z, c: (x, yh, yl, z, 1 - c))


def send(value, perm):
    return lax.ppermute(value, AXES, perm)


def add(*terms):
    total = terms[0].astype(F32)
    for term in terms[1:]:
        total = total + term.astype(F32)
    return total.astype(BF)


def dot(a, b, dims):
    return lax.dot_general(a, b, (dims, ((), ())), preferred_element_type=F32)


def per_device(hidden, weight, grad_out):
    row, col = lax.axis_index("row"), lax.axis_index("col")
    core = col % 2
    x, y_hi = col // 2 % 4, col // 8
    z, y_lo = row // 2, row % 2
    s = 1 - 2 * core
    a = VIA_Y

    mine = lax.dynamic_slice_in_dim(grad_out, core * 128, 128, 0)
    theirs = lax.dynamic_slice_in_dim(grad_out, (1 - core) * 128, 128, 0)
    g = jnp.concatenate([mine, send(theirs, CORE)], axis=1)
    w = jnp.concatenate([weight, send(weight, CORE)], axis=1)
    g = jnp.concatenate([g, send(g, YL)], axis=0)
    g3, g1 = send(g, Z1), send(g, Z2)
    g2 = send(g3, Z1)
    g = jnp.concatenate([g, g1, g2, g3], axis=0).reshape(8, 128, 1024)
    order = []
    for j in range(8):
        r = (y_hi + j // 4) % 2 * 4 + (x + s * (j % 4)) % 4
        order.append(((r // 2 - z) * s) % 4 * 2 + (r + y_lo) % 2)
    g = jnp.concatenate(
        [lax.dynamic_index_in_dim(g, i, 0, keepdims=False) for i in order], axis=0
    )

    h0 = hidden
    h3, h1, k0 = send(h0, X1), send(h0, X2), send(h0, YH)
    h2 = send(h3, X1)
    k3b, k1b = send(k0[a:], X1), send(k0[a:], X2)
    k3a, k1a = send(h3[:a], YH), send(h1[:a], YH)
    k2b = send(k3b, X1)
    k2a = send(h2[:a], YH)
    h_near = jnp.concatenate([h0, h1, h2, h3], axis=0)
    h_far = jnp.concatenate([k0, k1a, k1b, k2a, k2b, k3a, k3b], axis=0)

    far = dot(g[512:], w, ((1,), (1,))).astype(BF).reshape(4, 128, 3328)
    near = dot(g[:512], w, ((1,), (1,))).astype(BF).reshape(4, 128, 3328)
    r3 = send(far[2, a:], X1)
    r2 = send(far[3, a:], X2)
    n2 = send(far[2, :a], YH)
    n1, n3 = send(far[1, :a], YH), send(far[3, :a], YH)
    r1 = send(add(far[1, a:], r3), X1)
    d3 = send(jnp.concatenate([add(near[2, :a], n2), near[2, a:]], axis=0), X1)
    d2 = send(jnp.concatenate([add(near[3, :a], n3), near[3, a:]], axis=0), X2)
    n0 = send(jnp.concatenate([far[0, :a], add(far[0, a:], r1, r2)], axis=0), YH)
    d1 = send(
        jnp.concatenate([add(near[1, :a], n1, d3[:a]), add(near[1, a:], d3[a:])], axis=0), X1
    )
    grad_hidden = add(near[0], n0, d1, d2)

    out = jnp.concatenate(
        [dot(h_near, w, ((1,), (0,))).astype(BF), dot(h_far, w, ((1,), (0,))).astype(BF)], axis=0
    ).reshape(8, 128, 1024)

    def rows_for(dz):
        picked = []
        for dy in range(2):
            r = (z + s * dz) % 4 * 2 + (y_lo + dy) % 2
            j = (r // 4 + y_hi) % 2 * 4 + ((r % 4 - x) * s) % 4
            picked.append(lax.dynamic_index_in_dim(out, j, 0, keepdims=False))
        return jnp.concatenate(picked, axis=0)

    o3, o2 = send(rows_for(2), Z1), send(rows_for(3), Z2)
    o1 = send(add(rows_for(1), o3), Z1)
    o = add(rows_for(0), o1, o2)
    o = add(o[:128], send(o[128:], YL))
    own, other = o[:, :512], send(o[:, 512:], CORE)
    output = jnp.where(
        core == 0, jnp.concatenate([own, other], axis=0), jnp.concatenate([other, own], axis=0)
    )

    h = jnp.concatenate([h_near, h_far], axis=0)
    v = send(dot(h, g[:, 512:], ((0,), (0,))).astype(BF), CORE)
    grad_weight = (dot(h, g[:, :512], ((0,), (0,))) + v.astype(F32)).astype(BF)
    return output, grad_hidden, grad_weight


def solution(mesh):
    placed = (P("col", "row"), P("row", "col"), P("row", "col"))
    return jax.shard_map(
        per_device,
        mesh=mesh,
        in_specs=placed,
        out_specs=(P("row", "col"), P("col", "row"), P("row", "col")),
        check_vma=False,
    )
```

```python
import jax
import jax.numpy as jnp
from jax import lax
from jax.experimental import pallas as pl
from jax.experimental.pallas import tpu as pltpu
from jax.sharding import PartitionSpec as P

BF, F32 = jnp.bfloat16, jnp.float32
AXES = ("row", "col")
GATHER_VIA_Y = 48
REDUCE_VIA_Y = 32


def place(row, col):
    z, y_lo = divmod(row, 2)
    y_hi, rest = divmod(col, 8)
    x, core = divmod(rest, 2)
    return x, y_hi, y_lo, z, core


def permutation(move):
    pairs = []
    for row in range(8):
        for col in range(16):
            x, y_hi, y_lo, z, core = move(*place(row, col))
            pairs.append((row * 16 + col, (z % 4 * 2 + y_lo) * 16 + y_hi * 8 + x % 4 * 2 + core))
    return pairs


X1 = permutation(lambda x, yh, yl, z, c: (x + 1 - 2 * c, yh, yl, z, c))
X2 = permutation(lambda x, yh, yl, z, c: (x - 1 + 2 * c, yh, yl, z, c))
Z1 = permutation(lambda x, yh, yl, z, c: (x, yh, yl, z + 1 - 2 * c, c))
Z2 = permutation(lambda x, yh, yl, z, c: (x, yh, yl, z - 1 + 2 * c, c))
YH = permutation(lambda x, yh, yl, z, c: (x, 1 - yh, yl, z, c))
YL = permutation(lambda x, yh, yl, z, c: (x, yh, 1 - yl, z, c))
CORE = permutation(lambda x, yh, yl, z, c: (x, yh, yl, z, 1 - c))


def send(value, perm):
    return lax.ppermute(value, AXES, perm)


def add(*terms):
    total = terms[0].astype(F32)
    for term in terms[1:]:
        total = total + term.astype(F32)
    return total.astype(BF)


def tie(*values):
    return lax.optimization_barrier(values)


def dot(a, b, dims):
    return lax.dot_general(a, b, (dims, ((), ())), preferred_element_type=F32)


def pick(blocks, order):
    def kernel(order_ref, blocks_ref, picked_ref):
        for j in range(len(order)):
            picked_ref[j] = blocks_ref[order_ref[j]]

    return pl.pallas_call(
        kernel,
        out_shape=jax.ShapeDtypeStruct((len(order), *blocks.shape[1:]), blocks.dtype),
        in_specs=[
            pl.BlockSpec(memory_space=pltpu.SMEM),
            pl.BlockSpec(memory_space=pltpu.VMEM),
        ],
        out_specs=pl.BlockSpec(memory_space=pltpu.VMEM),
        compiler_params=pltpu.CompilerParams(vmem_limit_bytes=12 << 20),
        cost_estimate=pl.CostEstimate(flops=0, bytes_accessed=2 * blocks.size, transcendentals=0),
    )(jnp.stack(order).astype(jnp.int32), blocks)


def per_device(hidden, weight, grad_out):
    row, col = lax.axis_index("row"), lax.axis_index("col")
    core = col % 2
    x, y_hi = col // 2 % 4, col // 8
    z, y_lo = row // 2, row % 2
    s = 1 - 2 * core
    a, b = GATHER_VIA_Y, REDUCE_VIA_Y

    h0 = hidden
    side = send(grad_out, YL)
    h3 = send(h0, X1)
    w_other = send(weight, CORE)
    g = jnp.concatenate([grad_out, side], axis=0)
    h0, h3, g, w_other = tie(h0, h3, g, w_other)
    g3, g1 = send(g, Z1), send(g, Z2)
    h1, h2, k0b = send(h0, X2), send(h3, X1), send(h0[a:], YH)
    g2 = send(g3, Z1)
    w = jnp.concatenate([weight, w_other], axis=1)
    h1, h2, k0b, g1, g2, w = tie(h1, h2, k0b, g1, g2, w)
    k3b, k1b = send(k0b, X1), send(k0b, X2)
    ka = send(jnp.concatenate([h0[:a], h1[:a], h2[:a], h3[:a]], axis=0), YH)
    g = jnp.concatenate([g, g1, g2, g3], axis=0).reshape(16, 128, 512)

    def order_of(which):
        t = 1 - 2 * which
        order = []
        for j in range(8):
            r = (y_hi + j // 4) % 2 * 4 + (x + t * (j % 4)) % 4
            order.append(((r // 2 - z) * s) % 4 * 4 + (r + y_lo) % 2 * 2 + which)
        return order

    picked = pick(g, order_of(core) + order_of(1 - core)).reshape(2048, 512)
    g = jnp.concatenate([picked[:1024], send(picked[1024:], CORE)], axis=1)

    far = dot(g[512:], w, ((1,), (1,))).astype(BF).reshape(4, 128, 3328)
    far, k3b, k1b, g, h0, k0b = tie(far, k3b, k1b, g, h0, k0b)
    k2b = send(k3b, X1)
    r3, r2 = send(far[2, b:], X1), send(far[3, b:], X2)
    n = send(far[:, :b].reshape(4 * b, 3328), YH).reshape(4, b, 3328)
    near = dot(g[:512], w, ((1,), (1,))).astype(BF).reshape(4, 128, 3328)
    h_near = jnp.concatenate([h0, h1, h2, h3], axis=0)
    r1 = add(far[1, b:], r3)
    r1, k0b = tie(r1, k0b)
    r1 = send(r1, X1)
    ka = ka.reshape(4, a, 3328)
    h_far = jnp.concatenate([ka[0], k0b, ka[1], k1b, ka[2], k2b, ka[3], k3b], axis=0)

    out = jnp.concatenate(
        [dot(h_near, w, ((1,), (0,))).astype(BF), dot(h_far, w, ((1,), (0,))).astype(BF)], axis=0
    )

    d3 = jnp.concatenate([add(near[2, :b], n[2]), near[2, b:]], axis=0)
    d2 = jnp.concatenate([add(near[3, :b], n[3]), near[3, b:]], axis=0)
    h = jnp.concatenate([h_near, h_far], axis=0)
    h, out, d3, d2 = tie(h, out, d3, d2)
    d3, d2 = send(d3, X1), send(d2, X2)
    n0 = send(add(far[0, b:], r1, r2), YH)

    d1 = jnp.concatenate([add(near[1, :b], n[1], d3[:b]), add(near[1, b:], d3[b:])], axis=0)
    d1 = send(d1, X1)
    order = [(r // 4 + y_hi) % 2 * 4 + ((r % 4 - x) * s) % 4 for r in range(8)]
    out = pick(out.reshape(8, 128, 1024), order)
    out = lax.all_to_all(out, "row", 0, 0, tiled=True)
    o = jnp.sum(out.astype(F32), axis=0).astype(BF)
    own, other = o[:, :512], send(o[:, 512:], CORE)
    output = jnp.where(
        core == 0, jnp.concatenate([own, other], axis=0), jnp.concatenate([other, own], axis=0)
    )

    v = send(dot(h, g[:, 512:], ((0,), (0,))).astype(BF), CORE)
    grad_weight = (dot(h, g[:, :512], ((0,), (0,))) + v.astype(F32)).astype(BF)
    grad_weight, d1 = tie(grad_weight, d1)
    grad_hidden = add(near[0], jnp.concatenate([n[0], n0], axis=0), d1, d2)
    return output, grad_hidden, grad_weight


def solution(mesh):
    placed = (P("col", "row"), P("row", "col"), P("row", "col"))
    return jax.shard_map(
        per_device,
        mesh=mesh,
        in_specs=placed,
        out_specs=(P("row", "col"), P("col", "row"), P("row", "col")),
        check_vma=False,
    )
```

```python
import jax
import jax.numpy as jnp
from jax import lax
from jax.experimental import pallas as pl
from jax.experimental.pallas import tpu as pltpu
from jax.sharding import PartitionSpec as P

BF, F32 = jnp.bfloat16, jnp.float32
AXES = ("row", "col")
GATHER_VIA_Y = 32
REDUCE_VIA_Y = 32


def place(row, col):
    z, y_lo = divmod(row, 2)
    y_hi, rest = divmod(col, 8)
    x, core = divmod(rest, 2)
    return x, y_hi, y_lo, z, core


def permutation(move):
    pairs = []
    for row in range(8):
        for col in range(16):
            x, y_hi, y_lo, z, core = move(*place(row, col))
            pairs.append((row * 16 + col, (z % 4 * 2 + y_lo) * 16 + y_hi * 8 + x % 4 * 2 + core))
    return pairs


X1 = permutation(lambda x, yh, yl, z, c: (x + 1 - 2 * c, yh, yl, z, c))
X2 = permutation(lambda x, yh, yl, z, c: (x - 1 + 2 * c, yh, yl, z, c))
Z1 = permutation(lambda x, yh, yl, z, c: (x, yh, yl, z + 1 - 2 * c, c))
Z2 = permutation(lambda x, yh, yl, z, c: (x, yh, yl, z - 1 + 2 * c, c))
YH = permutation(lambda x, yh, yl, z, c: (x, 1 - yh, yl, z, c))
YL = permutation(lambda x, yh, yl, z, c: (x, yh, 1 - yl, z, c))
CORE = permutation(lambda x, yh, yl, z, c: (x, yh, yl, z, 1 - c))


def send(value, perm):
    return lax.ppermute(value, AXES, perm)


def add(*terms):
    total = terms[0].astype(F32)
    for term in terms[1:]:
        total = total + term.astype(F32)
    return total.astype(BF)


def tie(*values):
    return lax.optimization_barrier(values)


def dot(a, b, dims):
    return lax.dot_general(a, b, (dims, ((), ())), preferred_element_type=F32)


def pick(blocks, order):
    def kernel(order_ref, blocks_ref, picked_ref):
        for j in range(len(order)):
            picked_ref[j] = blocks_ref[order_ref[j]]

    return pl.pallas_call(
        kernel,
        out_shape=jax.ShapeDtypeStruct((len(order), *blocks.shape[1:]), blocks.dtype),
        in_specs=[
            pl.BlockSpec(memory_space=pltpu.SMEM),
            pl.BlockSpec(memory_space=pltpu.VMEM),
        ],
        out_specs=pl.BlockSpec(memory_space=pltpu.VMEM),
        compiler_params=pltpu.CompilerParams(vmem_limit_bytes=12 << 20),
        cost_estimate=pl.CostEstimate(flops=0, bytes_accessed=2 * blocks.size, transcendentals=0),
    )(jnp.stack(order).astype(jnp.int32), blocks)


SMALL = pl.CostEstimate(flops=1 << 20, bytes_accessed=1 << 20, transcendentals=0)


def assemble(refs, plan, whole):
    for array, start, rows, to in plan:
        whole[pl.ds(to, rows), :] = refs[array][pl.ds(start, rows), :]


def project(arrays, plan, weight):
    n, depth, width, tile = len(arrays), arrays[0].shape[1], weight.shape[1], 256
    total = sum(rows for _, _, rows, _ in plan)

    def kernel(*refs):
        weight_ref, out_ref, whole = refs[n:]

        @pl.when(pl.program_id(0) == 0)
        def _():
            assemble(refs, plan, whole)

        out_ref[...] = jnp.dot(whole[...], weight_ref[...], preferred_element_type=F32).astype(BF)

    return pl.pallas_call(
        kernel,
        grid=(width // tile,),
        out_shape=jax.ShapeDtypeStruct((total, width), BF),
        in_specs=[pl.BlockSpec(a.shape, lambda t: (0, 0)) for a in arrays]
        + [pl.BlockSpec((depth, tile), lambda t: (0, t))],
        out_specs=pl.BlockSpec((total, tile), lambda t: (0, t)),
        scratch_shapes=[pltpu.VMEM((total, depth), BF)],
        compiler_params=pltpu.CompilerParams(vmem_limit_bytes=36 << 20),
        cost_estimate=pl.CostEstimate(
            flops=2 * total * depth * width, bytes_accessed=16 << 20, transcendentals=0
        ),
    )(*arrays, weight)


def sum_blocks(blocks):
    def kernel(blocks_ref, sum_ref):
        total = blocks_ref[0].astype(F32)
        for i in range(1, blocks.shape[0]):
            total = total + blocks_ref[i].astype(F32)
        sum_ref[...] = total.astype(BF)

    return pl.pallas_call(
        kernel,
        out_shape=jax.ShapeDtypeStruct(blocks.shape[1:], BF),
        in_specs=[pl.BlockSpec(memory_space=pltpu.VMEM)],
        out_specs=pl.BlockSpec(memory_space=pltpu.VMEM),
        compiler_params=pltpu.CompilerParams(vmem_limit_bytes=12 << 20),
        cost_estimate=pl.CostEstimate(flops=24 << 30, bytes_accessed=4 << 20, transcendentals=0),
    )(blocks)


def weight_gradient(arrays, plan, cotangent, others=None):
    n, width, columns = len(arrays), arrays[0].shape[1], cotangent.shape[1]
    total, tile = cotangent.shape[0], width // 2
    half = pl.BlockSpec((tile, columns), lambda t: (0, 0))

    def kernel(*refs):
        cotangent_ref, whole = refs[n], refs[-1]
        assemble(refs, plan, whole)
        result = dot(whole[...], cotangent_ref[...], ((0,), (0,)))
        for t in range(2):

            @pl.when(pl.program_id(0) == t)
            def _():
                if others is None:
                    refs[n + 1 + t][...] = result.astype(BF)
                else:
                    refs[n + 3][...] = (result + refs[n + 1 + t][...].astype(F32)).astype(BF)

    halves = [jax.ShapeDtypeStruct((tile, columns), BF)] * 2
    return pl.pallas_call(
        kernel,
        grid=(2,),
        out_shape=halves if others is None else jax.ShapeDtypeStruct((width, columns), BF),
        in_specs=[pl.BlockSpec((a.shape[0], tile), lambda t: (0, t)) for a in arrays]
        + [pl.BlockSpec((total, columns), lambda t: (0, 0))]
        + ([] if others is None else [half, half]),
        out_specs=[half, half]
        if others is None
        else pl.BlockSpec((tile, columns), lambda t: (t, 0)),
        scratch_shapes=[pltpu.VMEM((total, tile), BF)],
        compiler_params=pltpu.CompilerParams(vmem_limit_bytes=56 << 20),
        cost_estimate=SMALL,
    )(*arrays, cotangent, *(others or []))


def per_device(hidden, weight, grad_out):
    row, col = lax.axis_index("row"), lax.axis_index("col")
    core = col % 2
    x, y_hi = col // 2 % 4, col // 8
    z, y_lo = row // 2, row % 2
    s = 1 - 2 * core
    a, b = GATHER_VIA_Y, REDUCE_VIA_Y

    h0 = hidden
    side = send(grad_out, YL)
    h3 = send(h0, X1)
    w_other = send(weight, CORE)
    g = jnp.concatenate([grad_out, side], axis=0)
    h0, h3, g, w_other = tie(h0, h3, g, w_other)
    g3, g1 = send(g, Z1), send(g, Z2)
    h1, h2, k0b = send(h0, X2), send(h3, X1), send(h0[a:], YH)
    g2 = send(g3, Z1)
    w = jnp.concatenate([weight, w_other], axis=1)
    h1, h2, k0b, g1, g2, w = tie(h1, h2, k0b, g1, g2, w)
    k3b, k1b = send(k0b, X1), send(k0b, X2)
    ka = send(jnp.concatenate([h0[:a], h1[:a], h2[:a], h3[:a]], axis=0), YH)
    g = jnp.concatenate([g, g1, g2, g3], axis=0).reshape(16, 128, 512)

    def order_of(which):
        t = 1 - 2 * which
        order = []
        for j in range(8):
            r = (y_hi + j // 4) % 2 * 4 + (x + t * (j % 4)) % 4
            order.append(((r // 2 - z) * s) % 4 * 4 + (r + y_lo) % 2 * 2 + which)
        return order

    picked = pick(g, order_of(core) + order_of(1 - core)).reshape(2048, 512)
    g_own, g_other = picked[:1024], send(picked[1024:], CORE)
    g = jnp.concatenate([g_own, g_other], axis=1)

    far = dot(g[512:], w, ((1,), (1,))).astype(BF).reshape(4, 128, 3328)
    far, k3b, k1b, g, h0, k0b = tie(far, k3b, k1b, g, h0, k0b)
    k2b = send(k3b, X1)
    r3 = send(far[2, b:], X1)
    r2, k2b = tie(far[3, b:], k2b)
    r2 = send(r2, X2)
    n = send(far[:, :b].reshape(4 * b, 3328), YH).reshape(4, b, 3328)
    near = dot(g[:512], w, ((1,), (1,))).astype(BF).reshape(4, 128, 3328)
    r1 = add(far[1, b:], r3)
    r1, k0b = tie(r1, k0b)
    r1 = send(r1, X1)

    arrays = [h0, h1, h2, h3, ka, k0b, k1b, k2b, k3b]
    plan = [(i, 0, 128, 128 * i) for i in range(4)]
    plan += [(4, a * i, a, 512 + 128 * i) for i in range(4)]
    plan += [(5 + i, 0, 128 - a, 512 + 128 * i + a) for i in range(4)]
    out = project(arrays, plan, w)

    d3 = jnp.concatenate([add(near[2, :b], n[2]), near[2, b:]], axis=0)
    d2 = jnp.concatenate([add(near[3, :b], n[3]), near[3, b:]], axis=0)
    order = [(r // 4 + y_hi) % 2 * 4 + ((r % 4 - x) * s) % 4 for r in range(8)]
    out = pick(out.reshape(8, 128, 1024), order)
    n0 = add(far[0, b:], r1, r2)
    h0, out, d3, d2, n0 = tie(h0, out, d3, d2, n0)
    out = lax.all_to_all(out, "row", 0, 0, tiled=True)
    d3, d2, n0 = send(d3, X1), send(d2, X2), send(n0, YH)

    arrays[0] = h0
    v, u = weight_gradient(arrays, plan, g_other)
    d3, d2, n0, v, u, arrays[0] = tie(d3, d2, n0, v, u, h0)
    d1 = jnp.concatenate([add(near[1, :b], n[1], d3[:b]), add(near[1, b:], d3[b:])], axis=0)
    d1, v, u = send(d1, X1), send(v, CORE), send(u, CORE)
    grad_weight = weight_gradient(arrays, plan, g_own, [v, u])
    grad_weight, out = tie(grad_weight, out)
    o = sum_blocks(out)
    own, other = o[:, :512], send(o[:, 512:], CORE)
    output = jnp.where(
        core == 0, jnp.concatenate([own, other], axis=0), jnp.concatenate([other, own], axis=0)
    )

    grad_hidden = add(near[0], jnp.concatenate([n[0], n0], axis=0), d1, d2)
    return output, grad_hidden, grad_weight


def solution(mesh):
    placed = (P("col", "row"), P("row", "col"), P("row", "col"))
    return jax.shard_map(
        per_device,
        mesh=mesh,
        in_specs=placed,
        out_specs=(P("row", "col"), P("col", "row"), P("row", "col")),
        check_vma=False,
    )
```

```python
import jax
import jax.numpy as jnp
from jax import lax
from jax.experimental import pallas as pl
from jax.experimental.pallas import tpu as pltpu
from jax.sharding import PartitionSpec as P

BF, F32 = jnp.bfloat16, jnp.float32
AXES = ("row", "col")
GATHER_VIA_Y = 32
REDUCE_VIA_Y = 32


def place(row, col):
    z, y_lo = divmod(row, 2)
    y_hi, rest = divmod(col, 8)
    x, core = divmod(rest, 2)
    return x, y_hi, y_lo, z, core


def permutation(move):
    pairs = []
    for row in range(8):
        for col in range(16):
            x, y_hi, y_lo, z, core = move(*place(row, col))
            pairs.append((row * 16 + col, (z % 4 * 2 + y_lo) * 16 + y_hi * 8 + x % 4 * 2 + core))
    return pairs


X1 = permutation(lambda x, yh, yl, z, c: (x + 1 - 2 * c, yh, yl, z, c))
X2 = permutation(lambda x, yh, yl, z, c: (x - 1 + 2 * c, yh, yl, z, c))
Z1 = permutation(lambda x, yh, yl, z, c: (x, yh, yl, z + 1 - 2 * c, c))
Z2 = permutation(lambda x, yh, yl, z, c: (x, yh, yl, z - 1 + 2 * c, c))
YH = permutation(lambda x, yh, yl, z, c: (x, 1 - yh, yl, z, c))
YL = permutation(lambda x, yh, yl, z, c: (x, yh, 1 - yl, z, c))
CORE = permutation(lambda x, yh, yl, z, c: (x, yh, yl, z, 1 - c))


def send(value, perm):
    return lax.ppermute(value, AXES, perm)


def add(*terms):
    total = terms[0].astype(F32)
    for term in terms[1:]:
        total = total + term.astype(F32)
    return total.astype(BF)


def tie(*values):
    return lax.optimization_barrier(values)


def dot(a, b, dims):
    return lax.dot_general(a, b, (dims, ((), ())), preferred_element_type=F32)


def pick(blocks, order):
    def kernel(order_ref, blocks_ref, picked_ref):
        for j in range(len(order)):
            picked_ref[j] = blocks_ref[order_ref[j]]

    return pl.pallas_call(
        kernel,
        out_shape=jax.ShapeDtypeStruct((len(order), *blocks.shape[1:]), blocks.dtype),
        in_specs=[
            pl.BlockSpec(memory_space=pltpu.SMEM),
            pl.BlockSpec(memory_space=pltpu.VMEM),
        ],
        out_specs=pl.BlockSpec(memory_space=pltpu.VMEM),
        compiler_params=pltpu.CompilerParams(vmem_limit_bytes=12 << 20),
        cost_estimate=pl.CostEstimate(flops=0, bytes_accessed=2 * blocks.size, transcendentals=0),
    )(jnp.stack(order).astype(jnp.int32), blocks)


SMALL = pl.CostEstimate(flops=1 << 20, bytes_accessed=1 << 20, transcendentals=0)


def assemble(refs, plan, whole):
    for array, start, rows, to in plan:
        whole[pl.ds(to, rows), :] = refs[array][pl.ds(start, rows), :]


def project(arrays, plan, weight):
    n, depth, width, tile = len(arrays), arrays[0].shape[1], weight.shape[1], 256
    total = sum(rows for _, _, rows, _ in plan)

    def kernel(*refs):
        weight_ref, out_ref, whole = refs[n:]

        @pl.when(pl.program_id(0) == 0)
        def _():
            assemble(refs, plan, whole)

        out_ref[...] = jnp.dot(whole[...], weight_ref[...], preferred_element_type=F32).astype(BF)

    return pl.pallas_call(
        kernel,
        grid=(width // tile,),
        out_shape=jax.ShapeDtypeStruct((total, width), BF),
        in_specs=[pl.BlockSpec(a.shape, lambda t: (0, 0)) for a in arrays]
        + [pl.BlockSpec((depth, tile), lambda t: (0, t))],
        out_specs=pl.BlockSpec((total, tile), lambda t: (0, t)),
        scratch_shapes=[pltpu.VMEM((total, depth), BF)],
        compiler_params=pltpu.CompilerParams(vmem_limit_bytes=36 << 20),
        cost_estimate=pl.CostEstimate(
            flops=2 * total * depth * width, bytes_accessed=16 << 20, transcendentals=0
        ),
    )(*arrays, weight)


def sum_blocks(blocks):
    def kernel(blocks_ref, sum_ref):
        total = blocks_ref[0].astype(F32)
        for i in range(1, blocks.shape[0]):
            total = total + blocks_ref[i].astype(F32)
        sum_ref[...] = total.astype(BF)

    return pl.pallas_call(
        kernel,
        out_shape=jax.ShapeDtypeStruct(blocks.shape[1:], BF),
        in_specs=[pl.BlockSpec(memory_space=pltpu.VMEM)],
        out_specs=pl.BlockSpec(memory_space=pltpu.VMEM),
        compiler_params=pltpu.CompilerParams(vmem_limit_bytes=12 << 20),
        cost_estimate=pl.CostEstimate(flops=24 << 30, bytes_accessed=4 << 20, transcendentals=0),
    )(blocks)


def weight_gradient(arrays, plan, cotangent, others=None):
    n, width, columns = len(arrays), arrays[0].shape[1], cotangent.shape[1]
    total, tile = cotangent.shape[0], width // 2
    half = pl.BlockSpec((tile, columns), lambda t: (0, 0))

    def kernel(*refs):
        cotangent_ref, whole = refs[n], refs[-1]
        assemble(refs, plan, whole)
        result = dot(whole[...], cotangent_ref[...], ((0,), (0,)))
        for t in range(2):

            @pl.when(pl.program_id(0) == t)
            def _():
                if others is None:
                    refs[n + 1 + t][...] = result.astype(BF)
                else:
                    refs[n + 3][...] = (result + refs[n + 1 + t][...].astype(F32)).astype(BF)

    halves = [jax.ShapeDtypeStruct((tile, columns), BF)] * 2
    return pl.pallas_call(
        kernel,
        grid=(2,),
        out_shape=halves if others is None else jax.ShapeDtypeStruct((width, columns), BF),
        in_specs=[pl.BlockSpec((a.shape[0], tile), lambda t: (0, t)) for a in arrays]
        + [pl.BlockSpec((total, columns), lambda t: (0, 0))]
        + ([] if others is None else [half, half]),
        out_specs=[half, half]
        if others is None
        else pl.BlockSpec((tile, columns), lambda t: (t, 0)),
        scratch_shapes=[pltpu.VMEM((total, tile), BF)],
        compiler_params=pltpu.CompilerParams(vmem_limit_bytes=56 << 20),
        cost_estimate=SMALL,
    )(*arrays, cotangent, *(others or []))


def per_device(hidden, weight, grad_out):
    row, col = lax.axis_index("row"), lax.axis_index("col")
    core = col % 2
    x, y_hi = col // 2 % 4, col // 8
    z, y_lo = row // 2, row % 2
    s = 1 - 2 * core
    a, b = GATHER_VIA_Y, REDUCE_VIA_Y

    h0 = hidden
    side = send(grad_out, YL)
    h3 = send(h0, X1)
    w_other = send(weight, CORE)
    g = jnp.concatenate([grad_out, side], axis=0)
    h0, h3, g, w_other = tie(h0, h3, g, w_other)
    g3, g1 = send(g, Z1), send(g, Z2)
    h1, h2, k0b = send(h0, X2), send(h3, X1), send(h0[a:], YH)
    g2 = send(g3, Z1)
    w = jnp.concatenate([weight, w_other], axis=1)
    h1, h2, k0b, g1, g2, w = tie(h1, h2, k0b, g1, g2, w)
    k3b, k1b = send(k0b, X1), send(k0b, X2)
    ka = send(jnp.concatenate([h0[:a], h1[:a], h2[:a], h3[:a]], axis=0), YH)
    g = jnp.concatenate([g, g1, g2, g3], axis=0).reshape(16, 128, 512)

    def order_of(which):
        t = 1 - 2 * which
        order = []
        for j in range(8):
            r = (y_hi + j // 4) % 2 * 4 + (x + t * (j % 4)) % 4
            order.append(((r // 2 - z) * s) % 4 * 4 + (r + y_lo) % 2 * 2 + which)
        return order

    g_other = send(pick(g, order_of(1 - core)).reshape(1024, 512), CORE)
    g_own = pick(g, order_of(core)).reshape(1024, 512)
    g = jnp.concatenate([g_own, g_other], axis=1)

    far = dot(g[512:], w, ((1,), (1,))).astype(BF).reshape(4, 128, 3328)
    far, k3b, k1b, g, h0, k0b = tie(far, k3b, k1b, g, h0, k0b)
    k2b = send(k3b, X1)
    r3 = send(far[2, b:], X1)
    r2, k2b = tie(far[3, b:], k2b)
    r2 = send(r2, X2)
    n = send(far[:, :b].reshape(4 * b, 3328), YH).reshape(4, b, 3328)
    near = dot(g[:512], w, ((1,), (1,))).astype(BF).reshape(4, 128, 3328)
    r1 = add(far[1, b:], r3)

    arrays = [h0, h1, h2, h3, ka, k0b, k1b, k2b, k3b]
    plan = [(i, 0, 128, 128 * i) for i in range(4)]
    plan += [(4, a * i, a, 512 + 128 * i) for i in range(4)]
    plan += [(5 + i, 0, 128 - a, 512 + 128 * i + a) for i in range(4)]
    out = project(arrays, plan, w)
    r1, out = tie(r1, out)
    r1 = send(r1, X1)

    d3 = jnp.concatenate([add(near[2, :b], n[2]), near[2, b:]], axis=0)
    d2 = jnp.concatenate([add(near[3, :b], n[3]), near[3, b:]], axis=0)
    order = [(r // 4 + y_hi) % 2 * 4 + ((r % 4 - x) * s) % 4 for r in range(8)]
    out = pick(out.reshape(8, 128, 1024), order)
    h0, out, d3, d2 = tie(h0, out, d3, d2)
    out = lax.all_to_all(out, "row", 0, 0, tiled=True)
    d3, d2 = send(d3, X1), send(d2, X2)
    n0 = send(add(far[0, b:], r1, r2), YH)

    arrays[0] = h0
    v, u = weight_gradient(arrays, plan, g_other)
    d3, d2, n0, v, u, arrays[0] = tie(d3, d2, n0, v, u, h0)
    d1 = jnp.concatenate([add(near[1, :b], n[1], d3[:b]), add(near[1, b:], d3[b:])], axis=0)
    d1, v, u = send(d1, X1), send(v, CORE), send(u, CORE)
    grad_weight = weight_gradient(arrays, plan, g_own, [v, u])
    grad_weight, out = tie(grad_weight, out)
    o = sum_blocks(out)
    own, other = o[:, :512], send(o[:, 512:], CORE)
    output = jnp.where(
        core == 0, jnp.concatenate([own, other], axis=0), jnp.concatenate([other, own], axis=0)
    )

    grad_hidden = add(near[0], jnp.concatenate([n[0], n0], axis=0), d1, d2)
    return output, grad_hidden, grad_weight


def solution(mesh):
    placed = (P("col", "row"), P("row", "col"), P("row", "col"))
    return jax.shard_map(
        per_device,
        mesh=mesh,
        in_specs=placed,
        out_specs=(P("row", "col"), P("col", "row"), P("row", "col")),
        check_vma=False,
    )
```

```python
import jax
import jax.numpy as jnp
from jax import lax
from jax.experimental import pallas as pl
from jax.experimental.pallas import tpu as pltpu
from jax.sharding import PartitionSpec as P

BF, F32 = jnp.bfloat16, jnp.float32
AXES = ("row", "col")
GATHER_VIA_Y = 32
REDUCE_VIA_Y = 32


def place(row, col):
    z, y_lo = divmod(row, 2)
    y_hi, rest = divmod(col, 8)
    x, core = divmod(rest, 2)
    return x, y_hi, y_lo, z, core


def permutation(move):
    pairs = []
    for row in range(8):
        for col in range(16):
            x, y_hi, y_lo, z, core = move(*place(row, col))
            pairs.append((row * 16 + col, (z % 4 * 2 + y_lo) * 16 + y_hi * 8 + x % 4 * 2 + core))
    return pairs


X1 = permutation(lambda x, yh, yl, z, c: (x + 1 - 2 * c, yh, yl, z, c))
X2 = permutation(lambda x, yh, yl, z, c: (x - 1 + 2 * c, yh, yl, z, c))
Z1 = permutation(lambda x, yh, yl, z, c: (x, yh, yl, z + 1 - 2 * c, c))
Z2 = permutation(lambda x, yh, yl, z, c: (x, yh, yl, z - 1 + 2 * c, c))
YH = permutation(lambda x, yh, yl, z, c: (x, 1 - yh, yl, z, c))
YL = permutation(lambda x, yh, yl, z, c: (x, yh, 1 - yl, z, c))
CORE = permutation(lambda x, yh, yl, z, c: (x, yh, yl, z, 1 - c))


def send(value, perm):
    return lax.ppermute(value, AXES, perm)


def add(*terms):
    total = terms[0].astype(F32)
    for term in terms[1:]:
        total = total + term.astype(F32)
    return total.astype(BF)


def tie(*values):
    return lax.optimization_barrier(values)


def dot(a, b, dims):
    return lax.dot_general(a, b, (dims, ((), ())), preferred_element_type=F32)


def pick(blocks, order):
    def kernel(order_ref, blocks_ref, picked_ref):
        for j in range(len(order)):
            picked_ref[j] = blocks_ref[order_ref[j]]

    return pl.pallas_call(
        kernel,
        out_shape=jax.ShapeDtypeStruct((len(order), *blocks.shape[1:]), blocks.dtype),
        in_specs=[
            pl.BlockSpec(memory_space=pltpu.SMEM),
            pl.BlockSpec(memory_space=pltpu.VMEM),
        ],
        out_specs=pl.BlockSpec(memory_space=pltpu.VMEM),
        compiler_params=pltpu.CompilerParams(vmem_limit_bytes=12 << 20),
        cost_estimate=pl.CostEstimate(flops=0, bytes_accessed=2 * blocks.size, transcendentals=0),
    )(jnp.stack(order).astype(jnp.int32), blocks)


SMALL = pl.CostEstimate(flops=1 << 20, bytes_accessed=1 << 20, transcendentals=0)


def assemble(refs, plan, whole):
    for array, start, rows, to in plan:
        whole[pl.ds(to, rows), :] = refs[array][pl.ds(start, rows), :]


def project(arrays, plan, weight):
    n, depth, width, tile = len(arrays), arrays[0].shape[1], weight.shape[1], 256
    total = sum(rows for _, _, rows, _ in plan)

    def kernel(*refs):
        weight_ref, out_ref, whole = refs[n:]

        @pl.when(pl.program_id(0) == 0)
        def _():
            assemble(refs, plan, whole)

        out_ref[...] = jnp.dot(whole[...], weight_ref[...], preferred_element_type=F32).astype(BF)

    return pl.pallas_call(
        kernel,
        grid=(width // tile,),
        out_shape=jax.ShapeDtypeStruct((total, width), BF),
        in_specs=[pl.BlockSpec(a.shape, lambda t: (0, 0)) for a in arrays]
        + [pl.BlockSpec((depth, tile), lambda t: (0, t))],
        out_specs=pl.BlockSpec((total, tile), lambda t: (0, t)),
        scratch_shapes=[pltpu.VMEM((total, depth), BF)],
        compiler_params=pltpu.CompilerParams(vmem_limit_bytes=36 << 20),
        cost_estimate=pl.CostEstimate(
            flops=2 * total * depth * width, bytes_accessed=16 << 20, transcendentals=0
        ),
    )(*arrays, weight)


def sum_blocks(blocks):
    def kernel(blocks_ref, sum_ref):
        total = blocks_ref[0].astype(F32)
        for i in range(1, blocks.shape[0]):
            total = total + blocks_ref[i].astype(F32)
        sum_ref[...] = total.astype(BF)

    return pl.pallas_call(
        kernel,
        out_shape=jax.ShapeDtypeStruct(blocks.shape[1:], BF),
        in_specs=[pl.BlockSpec(memory_space=pltpu.VMEM)],
        out_specs=pl.BlockSpec(memory_space=pltpu.VMEM),
        compiler_params=pltpu.CompilerParams(vmem_limit_bytes=12 << 20),
        cost_estimate=pl.CostEstimate(flops=24 << 30, bytes_accessed=4 << 20, transcendentals=0),
    )(blocks)


def weight_gradient(arrays, plan, cotangent, others=None):
    n, width, columns = len(arrays), arrays[0].shape[1], cotangent.shape[1]
    total, tile = cotangent.shape[0], width // 2
    half = pl.BlockSpec((tile, columns), lambda t: (0, 0))

    def kernel(*refs):
        cotangent_ref, whole = refs[n], refs[-1]
        assemble(refs, plan, whole)
        result = dot(whole[...], cotangent_ref[...], ((0,), (0,)))
        for t in range(2):

            @pl.when(pl.program_id(0) == t)
            def _():
                if others is None:
                    refs[n + 1 + t][...] = result.astype(BF)
                else:
                    refs[n + 3][...] = (result + refs[n + 1 + t][...].astype(F32)).astype(BF)

    halves = [jax.ShapeDtypeStruct((tile, columns), BF)] * 2
    return pl.pallas_call(
        kernel,
        grid=(2,),
        out_shape=halves if others is None else jax.ShapeDtypeStruct((width, columns), BF),
        in_specs=[pl.BlockSpec((a.shape[0], tile), lambda t: (0, t)) for a in arrays]
        + [pl.BlockSpec((total, columns), lambda t: (0, 0))]
        + ([] if others is None else [half, half]),
        out_specs=[half, half]
        if others is None
        else pl.BlockSpec((tile, columns), lambda t: (t, 0)),
        scratch_shapes=[pltpu.VMEM((total, tile), BF)],
        compiler_params=pltpu.CompilerParams(vmem_limit_bytes=56 << 20),
        cost_estimate=SMALL,
    )(*arrays, cotangent, *(others or []))


def per_device(hidden, weight, grad_out):
    row, col = lax.axis_index("row"), lax.axis_index("col")
    core = col % 2
    x, y_hi = col // 2 % 4, col // 8
    z, y_lo = row // 2, row % 2
    s = 1 - 2 * core
    a, b = GATHER_VIA_Y, REDUCE_VIA_Y

    h0 = hidden
    side = send(grad_out, YL)
    h3 = send(h0, X1)
    w_other = send(weight, CORE)
    g = jnp.concatenate([grad_out, side], axis=0)
    h0, g, w_other = tie(h0, g, w_other)
    g3, g1 = send(g, Z1), send(g, Z2)
    h1, h2, k0b = send(hidden, X2), send(h3, X1), send(h0[a:], YH)
    g3, g1 = tie(g3, g1)
    g2 = send(g3, Z1)
    w = jnp.concatenate([weight, w_other], axis=1)
    h1, h2, k0b, g1, g2, w = tie(h1, h2, k0b, g1, g2, w)
    k3b, k1b = send(k0b, X1), send(k0b, X2)
    ka = send(jnp.concatenate([h0[:a], h1[:a], h2[:a], h3[:a]], axis=0), YH)
    g = jnp.concatenate([g, g1, g2, g3], axis=0).reshape(16, 128, 512)

    def order_of(which):
        t = 1 - 2 * which
        order = []
        for j in range(8):
            r = (y_hi + j // 4) % 2 * 4 + (x + t * (j % 4)) % 4
            order.append(((r // 2 - z) * s) % 4 * 4 + (r + y_lo) % 2 * 2 + which)
        return order

    g_other = send(pick(g, order_of(1 - core)).reshape(1024, 512), CORE)
    g_own = pick(g, order_of(core)).reshape(1024, 512)
    g = jnp.concatenate([g_own, g_other], axis=1)

    far = dot(g[512:], w, ((1,), (1,))).astype(BF).reshape(4, 128, 3328)
    far, k3b, k1b, g, h0, k0b = tie(far, k3b, k1b, g, h0, k0b)
    k2b = send(k3b, X1)
    r3 = send(far[2, b:], X1)
    r2, k2b = tie(far[3, b:], k2b)
    r2 = send(r2, X2)
    n = send(far[:, :b].reshape(4 * b, 3328), YH).reshape(4, b, 3328)
    near = dot(g[:512], w, ((1,), (1,))).astype(BF).reshape(4, 128, 3328)
    r1 = add(far[1, b:], r3)

    arrays = [h0, h1, h2, h3, ka, k0b, k1b, k2b, k3b]
    plan = [(i, 0, 128, 128 * i) for i in range(4)]
    plan += [(4, a * i, a, 512 + 128 * i) for i in range(4)]
    plan += [(5 + i, 0, 128 - a, 512 + 128 * i + a) for i in range(4)]
    out = project(arrays, plan, w)
    r1, out = tie(r1, out)
    r1 = send(r1, X1)

    d3 = jnp.concatenate([add(near[2, :b], n[2]), near[2, b:]], axis=0)
    d2 = jnp.concatenate([add(near[3, :b], n[3]), near[3, b:]], axis=0)
    order = [(r // 4 + y_hi) % 2 * 4 + ((r % 4 - x) * s) % 4 for r in range(8)]
    out = pick(out.reshape(8, 128, 1024), order)
    h0, out, d3, d2 = tie(h0, out, d3, d2)
    out = lax.all_to_all(out, "row", 0, 0, tiled=True)
    d3, d2 = send(d3, X1), send(d2, X2)
    n0 = add(far[0, b:], r1, r2)

    arrays[0] = h0
    v, u = weight_gradient(arrays, plan, g_other)
    d3, d2, n0, v, u, arrays[0] = tie(d3, d2, n0, v, u, h0)
    d1 = jnp.concatenate([add(near[1, :b], n[1], d3[:b]), add(near[1, b:], d3[b:])], axis=0)
    n0, d1, v, u = send(n0, YH), send(d1, X1), send(v, CORE), send(u, CORE)
    grad_weight = weight_gradient(arrays, plan, g_own, [v, u])
    grad_weight, out, n0 = tie(grad_weight, out, n0)
    o = sum_blocks(out)
    own, other = o[:, :512], send(o[:, 512:], CORE)
    output = jnp.where(
        core == 0, jnp.concatenate([own, other], axis=0), jnp.concatenate([other, own], axis=0)
    )

    grad_hidden = add(near[0], jnp.concatenate([n[0], n0], axis=0), d1, d2)
    return output, grad_hidden, grad_weight


def solution(mesh):
    placed = (P("col", "row"), P("row", "col"), P("row", "col"))
    return jax.shard_map(
        per_device,
        mesh=mesh,
        in_specs=placed,
        out_specs=(P("row", "col"), P("col", "row"), P("row", "col")),
        check_vma=False,
    )
```
